512 devices in a mesh: mode: 8 (over y, core), col: 64 (over z, x).
Axes of the slice: x: 4, y: 4, z: 16, core: 2. Of those that a mesh axis runs over, the one named last changes fastest.
Arguments:
- tensor: float32 [512, 64, 4096], P('mode', 'col'), may hold values from -15 to 15
- start_basis: float32 [512, 128], replicated, may hold values from -6 to 6
Outputs:
- factor: float32 [512, 512], replicated
- basis: float32 [512, 128], replicated
- core: float32 [128, 64, 4096], P(None, 'col', 'mode')
The draws below stay inside these ranges and needn't reach their ends.
All inputs are finite; a program needn't handle non-finite values.
Results may differ from the reference program's by a relative error of at most 0.00018.
Values sent between devices are 32-bit elements; how exact they have to be, the bound alone decides.
No kernel may reach another device: no remote copies, remote signals or barrier semaphores. Data moves between devices by JAX's collectives and lax.ppermute only.
A program may use at most 64 MiB of HBM per device.

```python
import math
import jax
import jax.numpy as jnp
from jax import lax

I1 = 512
RANK = 128
J_LEN = 4096
POWER = 2
I2_LEN = 64


def draw_tensor(key, part):
    scale_key = jax.random.fold_in(key, 11)
    value_key = jax.random.fold_in(key, 23)
    scales = jnp.exp(jax.random.uniform(scale_key, (I1, 1, 1), jnp.float32, 0.0, math.log(2.0)))
    values = jnp.clip(jax.random.normal(value_key, (I1, I2_LEN, J_LEN), jnp.float32), -6.0, 6.0)
    return (scales * values).astype(jnp.float32)


def centred(rng, dims, width, reach, held_as=jnp.bfloat16):
    drawn = jax.random.normal(rng, dims, jnp.float32) * width
    return jnp.minimum(jnp.maximum(drawn, -reach), reach).astype(held_as)


def setup_inputs(seed: int = 0) -> dict:
    arg_keys = jax.random.split(jax.random.key(seed), 3)
    return {
        "tensor": draw_tensor(jax.random.fold_in(arg_keys[2], 71), 0),
        "start_basis": centred(arg_keys[1], (I1, RANK), 1.0, 6.0, jnp.float32),
    }


def lower_chol(matrix):
    return jnp.linalg.cholesky(matrix)

def orthonormal(image):
    small = lower_chol(jnp.dot(image.T.astype(jnp.float32), image.astype(jnp.float32), precision=lax.Precision.HIGHEST, preferred_element_type=jnp.float32))
    return jax.scipy.linalg.solve_triangular(small, image.T, lower=True).T

def reference(tensor, start_basis):
    unfolded = tensor.reshape(I1, -1)
    columns = unfolded.shape[1]
    gram = jnp.dot(unfolded.astype(jnp.float32), unfolded.T.astype(jnp.float32), precision=lax.Precision.HIGHEST, preferred_element_type=jnp.float32)
    factor = lower_chol(gram / columns)
    basis = start_basis
    for step in range(POWER):
        inner = jnp.dot(factor.T.astype(jnp.float32), basis.astype(jnp.float32), precision=lax.Precision.HIGHEST, preferred_element_type=jnp.float32)
        image = jnp.dot(factor.astype(jnp.float32), inner.astype(jnp.float32), precision=lax.Precision.HIGHEST, preferred_element_type=jnp.float32)
        basis = orthonormal(image)
    core = jnp.dot(basis.T.astype(jnp.float32), unfolded.astype(jnp.float32), precision=lax.Precision.HIGHEST, preferred_element_type=jnp.float32)
    return (factor, basis, core.reshape(RANK, I2_LEN, J_LEN))
```

```python
import jax
import jax.numpy as jnp
from jax import lax
from jax.experimental import pallas as pl
from jax.experimental.pallas import tpu as pltpu
from jax.sharding import Mesh, PartitionSpec as P

POWER = 2
LANES = 128
BLOCKS = [(r, c) for r in range(4) for c in range(r + 1)]


def matmul(left, right):
    return jnp.dot(left, right, precision=lax.Precision.HIGHEST, preferred_element_type=jnp.float32)


def orthonormal(image):
    small = jnp.linalg.cholesky(matmul(image.T, image))
    return jax.scipy.linalg.solve_triangular(small, image.T, lower=True).T


def split_kernel(x_ref, o_ref):
    for d in range(8):
        for c in range(4):
            o_ref[d, :, c * LANES : (c + 1) * LANES] = x_ref[pl.ds(d * 4 + c, 64, stride=32), :]


def split_columns(tensor):
    flat = tensor.reshape(64 * 32, LANES)
    return pl.pallas_call(
        split_kernel,
        out_shape=jax.ShapeDtypeStruct((8, 64, 512), jnp.float32),
    )(flat)


def dot_t(left, right):
    return lax.dot_general(left, right, (((1,), (1,)), ((), ())), preferred_element_type=jnp.float32)


def gram_kernel(f_ref, o_ref):
    full = f_ref[...]
    high = full.astype(jnp.bfloat16)
    low = (full - high.astype(jnp.float32)).astype(jnp.bfloat16)
    for r in range(4):
        rows = slice(r * LANES, (r + 1) * LANES)
        n = (r + 1) * LANES
        part = dot_t(high[rows], high[:n]) + dot_t(high[rows], low[:n]) + dot_t(low[rows], high[:n])
        for c in range(r + 1):
            start = BLOCKS.index((r, c)) * LANES
            o_ref[start : start + LANES, :] = part[:, c * LANES : (c + 1) * LANES]


def packed_gram(flat):
    return pl.pallas_call(
        gram_kernel,
        out_shape=jax.ShapeDtypeStruct((len(BLOCKS) * LANES, LANES), jnp.float32),
    )(flat)


def total_sum(packed):
    rows = packed.shape[0]
    own = lax.all_to_all(packed.reshape(32, rows // 32, LANES), ("mode", "x"), 0, 0, tiled=True).sum(0)
    own = jnp.pad(own, ((0, 8), (0, 0))).reshape(16, 3, LANES)
    own = lax.all_to_all(own, "z", 0, 0, tiled=True).sum(0)
    own = lax.all_to_all(jnp.broadcast_to(own, (16, 3, LANES)), "z", 0, 0, tiled=True)
    own = own.reshape(48, LANES)[: rows // 32]
    own = lax.all_to_all(jnp.broadcast_to(own, (32, *own.shape)), ("mode", "x"), 0, 0, tiled=True)
    return own.reshape(rows, LANES)


def unpack(packed):
    blocks = {b: packed[i * LANES : (i + 1) * LANES] for i, b in enumerate(BLOCKS)}
    return jnp.block([[blocks[(r, c)] if r >= c else blocks[(c, r)].T for c in range(4)] for r in range(4)])


def per_device(tensor, start_basis):
    regrouped = lax.all_to_all(split_columns(tensor), "mode", 0, 0, tiled=True)
    flat = regrouped.reshape(512, 512)
    scaled = unpack(total_sum(packed_gram(flat))) / 262144
    factor = jnp.linalg.cholesky(scaled)
    basis = start_basis
    for step in range(POWER):
        basis = orthonormal(matmul(scaled, basis))
    core = matmul(basis.T, flat).reshape(128, 1, 512)
    return (factor, basis, core)


def solution(mesh):
    grid = Mesh(mesh.devices.reshape(8, 16, 4), ("mode", "z", "x"))
    in_specs = (P("mode", ("z", "x"), None), P())
    out_specs = (P(), P(), P(None, ("z", "x"), "mode"))
    return jax.shard_map(
        per_device, mesh=grid, in_specs=in_specs, out_specs=out_specs, check_vma=False
    )
```

```python
import functools

import jax
import jax.numpy as jnp
from jax import lax
from jax.experimental import pallas as pl
from jax.experimental.pallas import tpu as pltpu
from jax.sharding import Mesh, PartitionSpec as P

LANES = 128
BLOCKS = [(r, c) for r in range(4) for c in range(r + 1)]
HIGHEST = lax.Precision.HIGHEST


def three(x):
    high = x.astype(jnp.bfloat16)
    rest = x - high.astype(jnp.float32)
    mid = rest.astype(jnp.bfloat16)
    low = (rest - mid.astype(jnp.float32)).astype(jnp.bfloat16)
    return high, mid, low


def stack(x):
    h, m, l = three(x)
    return jnp.concatenate([h, h, m, h, l, m], 0), jnp.concatenate([h, m, h, l, h, m], 0)


def dot_tn(left, right):
    return lax.dot_general(left, right, (((0,), (0,)), ((), ())), preferred_element_type=jnp.float32)


def lane(x, index):
    return jnp.take_along_axis(x, index, axis=1)


def row(x, k):
    return jnp.broadcast_to(x[k : k + 1, :], (8, LANES))


def eliminate(diag, groups, base):
    nv = len(groups[0])
    diag, groups = list(diag), [list(g) for g in groups]
    zero = jnp.zeros((8, LANES), jnp.int32) + base
    done = []
    for j in range(4):
        cols = {i: [lane(diag[i], zero + (8 * j + k)) for k in range(8)] for i in range(j, 4)}
        a = {(m, k): row(cols[j][k], m) for k in range(8) for m in range(k, 8)}
        scale, rows, drows = [], [], []
        for k in range(8):
            r = lax.rsqrt(a[k, k])
            scale.append(r)
            low = {m: a[m, k] * r for m in range(k + 1, 8)}
            for m in range(k + 1, 8):
                for q in range(k + 1, m + 1):
                    a[m, q] = a[m, q] - low[m] * low[q]
                a[m, k] = low[m]
        for i in range(j + 1, 4):
            for k in range(8):
                c = cols[i][k]
                for m in range(k):
                    c = c - cols[i][m] * a[k, m]
                cols[i][k] = c * scale[k]
        for k in range(8):
            d = row(diag[j], k)
            g = [row(groups[j][v], k) for v in range(nv)]
            for m in range(k):
                d = d - a[k, m] * drows[m]
                g = [g[v] - a[k, m] * rows[m][v] for v in range(nv)]
            drows.append(d * scale[k])
            rows.append([x * scale[k] for x in g])
        for i in range(j + 1, 4):
            for k in range(8):
                diag[i] = diag[i] - cols[i][k] * drows[k]
                groups[i] = [groups[i][v] - cols[i][k] * rows[k][v] for v in range(nv)]
        done += rows
    return done


def chain_kernel(g_ref, x_ref, f_ref, fac_ref, basis_ref, core_ref, w, a_full, u, aug, ub, us, ubs, left, right):
    inv = 1.0 / 262144
    for i, (r, c) in enumerate(BLOCKS):
        block = g_ref[i * LANES : (i + 1) * LANES, :] * inv
        rs, cs = slice(r * LANES, (r + 1) * LANES), slice(c * LANES, (c + 1) * LANES)
        w[rs, cs] = block
        a_full[rs, cs] = block
        if r != c:
            flipped = block.T
            w[cs, rs] = flipped
            a_full[cs, rs] = flipped
    left[...] = jnp.zeros_like(left)
    right[...] = jnp.zeros_like(right)
    aug[:, LANES:] = x_ref[...].T

    def factor_step(s):
        block = s // 4
        base = lax.rem(s, 4) * 32
        start = pl.multiple_of(s * 32, 32)
        col = pl.multiple_of(block * LANES, LANES)
        diag = [w[pl.ds(start + 8 * i, 8), pl.ds(col, LANES)] for i in range(4)]
        groups = [[w[pl.ds(start + 8 * i, 8), v * LANES : (v + 1) * LANES] for v in range(4)] for i in range(4)]
        lft, rgt = left, right
        for q in range(1, 4):
            other = pl.multiple_of(lax.rem(block + q, 4) * LANES, LANES)
            w[pl.ds(other, LANES), :] -= dot_tn(lft[:, pl.ds(other, LANES)], rgt[...])
        rows = eliminate(diag, groups, base)
        for k in range(32):
            for v in range(4):
                us[k : k + 1, v * LANES : (v + 1) * LANES] = rows[k][v][0:1]
        u[pl.ds(start, 32), :] = us[...]
        lf, rg = stack(us[...])
        left[...] = lf
        right[...] = rg
        nxt = pl.multiple_of(jnp.minimum((s + 1) // 4, 3) * LANES, LANES)
        w[pl.ds(nxt, LANES), :] -= dot_tn(left[:, pl.ds(nxt, LANES)], rg)

    def basis_step(q):
        start = pl.multiple_of(q * 32, 32)
        groups = [[aug[pl.ds(start + 8 * i, 8), v * LANES : (v + 1) * LANES] for v in range(5)] for i in range(4)]
        rows = eliminate([g[0] for g in groups], groups, q * 32)
        for k in range(32):
            for v in range(5):
                ubs[k : k + 1, v * LANES : (v + 1) * LANES] = rows[k][v][0:1]
        ub[pl.ds(start, 32), :] = ubs[...]
        lf, rg = stack(ubs[...])
        aug[...] -= dot_tn(lf[:, :LANES], rg)

    def power(t, carry):
        @pl.when(t > 0)
        def _():
            aug[:, LANES:] = ub[:, LANES:]
        image = jnp.dot(aug[:, LANES:], a_full[...], precision=HIGHEST, preferred_element_type=jnp.float32)
        aug[:, LANES:] = image
        aug[:, :LANES] = lax.dot_general(image, image, (((1,), (1,)), ((), ())), precision=HIGHEST, preferred_element_type=jnp.float32)

        def both(q, c):
            factor_step(4 * t + q)
            basis_step(q)
            return c
        return lax.fori_loop(0, 4, both, carry)

    lax.fori_loop(0, 2, power, 0)
    basis_t = ub[:, LANES:]
    basis_ref[...] = basis_t.T
    fh = f_ref[...].astype(jnp.bfloat16)
    fl = (f_ref[...] - fh.astype(jnp.float32)).astype(jnp.bfloat16)
    bh = basis_t.astype(jnp.bfloat16)
    bl = (basis_t - bh.astype(jnp.float32)).astype(jnp.bfloat16)
    dot = functools.partial(jnp.dot, preferred_element_type=jnp.float32)
    core = dot(bh, fh) + dot(bh, fl) + dot(bl, fh)
    for c in range(4):
        core_ref[pl.ds(c, LANES, stride=4), :] = core[:, c * LANES : (c + 1) * LANES]

    def rest(s, c):
        factor_step(s)
        return c
    lax.fori_loop(8, 16, rest, 0)
    for r in range(4):
        for c in range(4):
            rs, cs = slice(r * LANES, (r + 1) * LANES), slice(c * LANES, (c + 1) * LANES)
            if r < c:
                fac_ref[rs, cs] = jnp.zeros((LANES, LANES), jnp.float32)
            else:
                block = u[cs, rs]
                if r == c:
                    up = lax.broadcasted_iota(jnp.int32, (LANES, LANES), 0) <= lax.broadcasted_iota(jnp.int32, (LANES, LANES), 1)
                    block = jnp.where(up, block, 0.0)
                fac_ref[rs, cs] = block.T


def chain(packed, start_basis, flat):
    f32, b16 = jnp.float32, jnp.bfloat16
    return pl.pallas_call(
        chain_kernel,
        out_shape=(
            jax.ShapeDtypeStruct((512, 512), f32),
            jax.ShapeDtypeStruct((512, 128), f32),
            jax.ShapeDtypeStruct((512, 128), f32),
        ),
        scratch_shapes=[
            pltpu.VMEM((512, 512), f32), pltpu.VMEM((512, 512), f32), pltpu.VMEM((512, 512), f32),
            pltpu.VMEM((128, 640), f32), pltpu.VMEM((128, 640), f32),
            pltpu.VMEM((32, 512), f32), pltpu.VMEM((32, 640), f32),
            pltpu.VMEM((192, 512), b16), pltpu.VMEM((192, 512), b16),
        ],
        compiler_params=pltpu.CompilerParams(vmem_limit_bytes=48 * 2**20),
    )(packed, start_basis, flat)


def split_kernel(x_ref, o_ref):
    for d in range(8):
        for c in range(4):
            o_ref[d, :, c * LANES : (c + 1) * LANES] = x_ref[pl.ds(d * 4 + c, 64, stride=32), :]


def split_columns(tensor):
    flat = tensor.reshape(64 * 32, LANES)
    return pl.pallas_call(
        split_kernel,
        out_shape=jax.ShapeDtypeStruct((8, 64, 512), jnp.float32),
    )(flat)


def dot_t(left, right):
    return lax.dot_general(left, right, (((1,), (1,)), ((), ())), preferred_element_type=jnp.float32)


def gram_kernel(f_ref, o_ref):
    full = f_ref[...]
    high = full.astype(jnp.bfloat16)
    low = (full - high.astype(jnp.float32)).astype(jnp.bfloat16)
    for r in range(4):
        rows = slice(r * LANES, (r + 1) * LANES)
        n = (r + 1) * LANES
        part = dot_t(high[rows], high[:n]) + dot_t(high[rows], low[:n]) + dot_t(low[rows], high[:n])
        for c in range(r + 1):
            start = BLOCKS.index((r, c)) * LANES
            o_ref[start : start + LANES, :] = part[:, c * LANES : (c + 1) * LANES]


def packed_gram(flat):
    return pl.pallas_call(
        gram_kernel,
        out_shape=jax.ShapeDtypeStruct((len(BLOCKS) * LANES, LANES), jnp.float32),
    )(flat)


def total_sum(packed):
    rows = packed.shape[0]
    own = lax.all_to_all(packed.reshape(32, rows // 32, LANES), ("mode", "x"), 0, 0, tiled=True).sum(0)
    own = jnp.pad(own, ((0, 8), (0, 0))).reshape(16, 3, LANES)
    own = lax.all_to_all(own, "z", 0, 0, tiled=True).sum(0)
    own = lax.all_to_all(jnp.broadcast_to(own, (16, 3, LANES)), "z", 0, 0, tiled=True)
    own = own.reshape(48, LANES)[: rows // 32]
    own = lax.all_to_all(jnp.broadcast_to(own, (32, *own.shape)), ("mode", "x"), 0, 0, tiled=True)
    return own.reshape(rows, LANES)


def per_device(tensor, start_basis):
    regrouped = lax.all_to_all(split_columns(tensor), "mode", 0, 0, tiled=True)
    flat = regrouped.reshape(512, 512)
    factor, basis, core = chain(total_sum(packed_gram(flat)), start_basis, flat)
    return (factor, basis, core.reshape(128, 1, 512))


def solution(mesh):
    grid = Mesh(mesh.devices.reshape(8, 16, 4), ("mode", "z", "x"))
    in_specs = (P("mode", ("z", "x"), None), P())
    out_specs = (P(), P(), P(None, ("z", "x"), "mode"))
    return jax.shard_map(
        per_device, mesh=grid, in_specs=in_specs, out_specs=out_specs, check_vma=False
    )
```

```python
import functools

import jax
import jax.numpy as jnp
from jax import lax
from jax.experimental import pallas as pl
from jax.experimental.pallas import tpu as pltpu
from jax.sharding import Mesh, PartitionSpec as P

LANES = 128
BLOCKS = [(r, c) for r in range(4) for c in range(r + 1)]
HALF = len(BLOCKS) // 2
NEAR = ("y", "z_low", "x")
FAR = ("z_high",)
HIGHEST = lax.Precision.HIGHEST


def three(x):
    high = x.astype(jnp.bfloat16)
    rest = x - high.astype(jnp.float32)
    mid = rest.astype(jnp.bfloat16)
    low = (rest - mid.astype(jnp.float32)).astype(jnp.bfloat16)
    return high, mid, low


def stack(x):
    h, m, l = three(x)
    return jnp.concatenate([h, h, m, h, l, m], 0), jnp.concatenate([h, m, h, l, h, m], 0)


def dot_tn(left, right):
    return lax.dot_general(left, right, (((0,), (0,)), ((), ())), preferred_element_type=jnp.float32)


def lane(x, index):
    return jnp.take_along_axis(x, index, axis=1)


def row(x, k):
    return jnp.broadcast_to(x[k : k + 1, :], (8, LANES))


def eliminate(diag, groups, base):
    nv = len(groups[0])
    diag, groups = list(diag), [list(g) for g in groups]
    zero = jnp.zeros((8, LANES), jnp.int32) + base
    done = []
    for j in range(4):
        cols = {i: [lane(diag[i], zero + (8 * j + k)) for k in range(8)] for i in range(j, 4)}
        a = {(m, k): row(cols[j][k], m) for k in range(8) for m in range(k, 8)}
        scale, rows, drows = [], [], []
        for k in range(8):
            r = lax.rsqrt(a[k, k])
            scale.append(r)
            low = {m: a[m, k] * r for m in range(k + 1, 8)}
            for m in range(k + 1, 8):
                for q in range(k + 1, m + 1):
                    a[m, q] = a[m, q] - low[m] * low[q]
                a[m, k] = low[m]
        for i in range(j + 1, 4):
            for k in range(8):
                c = cols[i][k]
                for m in range(k):
                    c = c - cols[i][m] * a[k, m]
                cols[i][k] = c * scale[k]
        for k in range(8):
            d = row(diag[j], k)
            g = [row(groups[j][v], k) for v in range(nv)]
            for m in range(k):
                d = d - a[k, m] * drows[m]
                g = [g[v] - a[k, m] * rows[m][v] for v in range(nv)]
            drows.append(d * scale[k])
            rows.append([x * scale[k] for x in g])
        for i in range(j + 1, 4):
            for k in range(8):
                diag[i] = diag[i] - cols[i][k] * drows[k]
                groups[i] = [groups[i][v] - cols[i][k] * rows[k][v] for v in range(nv)]
        done += rows
    return done


def chain_kernel(mine_ref, other_ref, x_ref, f_ref, fac_ref, basis_ref, core_ref, w, a_full, u, aug, ub, us, ubs, left, right):
    core = lax.axis_index("core")
    for me in range(2):
        @pl.when(core == me)
        def _():
            for i, (r, c) in enumerate(BLOCKS):
                ref = mine_ref if i // HALF == me else other_ref
                block = ref[i % HALF * LANES : (i % HALF + 1) * LANES, :] * (1.0 / 262144)
                rs, cs = slice(r * LANES, (r + 1) * LANES), slice(c * LANES, (c + 1) * LANES)
                w[rs, cs] = block
                a_full[rs, cs] = block
                if r != c:
                    flipped = block.T
                    w[cs, rs] = flipped
                    a_full[cs, rs] = flipped
    left[...] = jnp.zeros_like(left)
    right[...] = jnp.zeros_like(right)
    aug[:, LANES:] = x_ref[...].T

    def factor_step(s):
        block = s // 4
        base = lax.rem(s, 4) * 32
        start = pl.multiple_of(s * 32, 32)
        col = pl.multiple_of(block * LANES, LANES)
        diag = [w[pl.ds(start + 8 * i, 8), pl.ds(col, LANES)] for i in range(4)]
        groups = [[w[pl.ds(start + 8 * i, 8), v * LANES : (v + 1) * LANES] for v in range(4)] for i in range(4)]
        lft, rgt = left, right
        for q in range(1, 4):
            other = pl.multiple_of(lax.rem(block + q, 4) * LANES, LANES)
            w[pl.ds(other, LANES), :] -= dot_tn(lft[:, pl.ds(other, LANES)], rgt[...])
        rows = eliminate(diag, groups, base)
        for k in range(32):
            for v in range(4):
                us[k : k + 1, v * LANES : (v + 1) * LANES] = rows[k][v][0:1]
        u[pl.ds(start, 32), :] = us[...]
        lf, rg = stack(us[...])
        left[...] = lf
        right[...] = rg
        nxt = pl.multiple_of(jnp.minimum((s + 1) // 4, 3) * LANES, LANES)
        w[pl.ds(nxt, LANES), :] -= dot_tn(left[:, pl.ds(nxt, LANES)], rg)

    def basis_step(q):
        start = pl.multiple_of(q * 32, 32)
        groups = [[aug[pl.ds(start + 8 * i, 8), v * LANES : (v + 1) * LANES] for v in range(5)] for i in range(4)]
        rows = eliminate([g[0] for g in groups], groups, q * 32)
        for k in range(32):
            for v in range(5):
                ubs[k : k + 1, v * LANES : (v + 1) * LANES] = rows[k][v][0:1]
        ub[pl.ds(start, 32), :] = ubs[...]
        lf, rg = stack(ubs[...])
        aug[...] -= dot_tn(lf[:, :LANES], rg)

    def power(t, carry):
        @pl.when(t > 0)
        def _():
            aug[:, LANES:] = ub[:, LANES:]
        image = jnp.dot(aug[:, LANES:], a_full[...], precision=HIGHEST, preferred_element_type=jnp.float32)
        aug[:, LANES:] = image
        aug[:, :LANES] = lax.dot_general(image, image, (((1,), (1,)), ((), ())), precision=HIGHEST, preferred_element_type=jnp.float32)

        def both(q, c):
            factor_step(4 * t + q)
            basis_step(q)
            return c
        return lax.fori_loop(0, 4, both, carry)

    lax.fori_loop(0, 2, power, 0)
    basis_t = ub[:, LANES:]
    basis_ref[...] = basis_t.T
    fh = f_ref[...].astype(jnp.bfloat16)
    fl = (f_ref[...] - fh.astype(jnp.float32)).astype(jnp.bfloat16)
    bh = basis_t.astype(jnp.bfloat16)
    bl = (basis_t - bh.astype(jnp.float32)).astype(jnp.bfloat16)
    dot = functools.partial(jnp.dot, preferred_element_type=jnp.float32)
    core = dot(bh, fh) + dot(bh, fl) + dot(bl, fh)
    for c in range(4):
        core_ref[pl.ds(c, LANES, stride=4), :] = core[:, c * LANES : (c + 1) * LANES]

    def rest(s, c):
        factor_step(s)
        return c
    lax.fori_loop(8, 16, rest, 0)
    for r in range(4):
        for c in range(4):
            rs, cs = slice(r * LANES, (r + 1) * LANES), slice(c * LANES, (c + 1) * LANES)
            if r < c:
                fac_ref[rs, cs] = jnp.zeros((LANES, LANES), jnp.float32)
            else:
                block = u[cs, rs]
                if r == c:
                    up = lax.broadcasted_iota(jnp.int32, (LANES, LANES), 0) <= lax.broadcasted_iota(jnp.int32, (LANES, LANES), 1)
                    block = jnp.where(up, block, 0.0)
                fac_ref[rs, cs] = block.T


def chain(mine, other, start_basis, flat):
    f32, b16 = jnp.float32, jnp.bfloat16
    return pl.pallas_call(
        chain_kernel,
        out_shape=(
            jax.ShapeDtypeStruct((512, 512), f32),
            jax.ShapeDtypeStruct((512, 128), f32),
            jax.ShapeDtypeStruct((512, 128), f32),
        ),
        scratch_shapes=[
            pltpu.VMEM((512, 512), f32), pltpu.VMEM((512, 512), f32), pltpu.VMEM((512, 512), f32),
            pltpu.VMEM((128, 640), f32), pltpu.VMEM((128, 640), f32),
            pltpu.VMEM((32, 512), f32), pltpu.VMEM((32, 640), f32),
            pltpu.VMEM((192, 512), b16), pltpu.VMEM((192, 512), b16),
        ],
        compiler_params=pltpu.CompilerParams(vmem_limit_bytes=24 * 2**20),
    )(mine, other, start_basis, flat)


def split_kernel(x_ref, o_ref):
    for d in range(8):
        for c in range(4):
            o_ref[d, :, c * LANES : (c + 1) * LANES] = x_ref[pl.ds(d * 4 + c, 64, stride=32), :]


def split_columns(tensor):
    flat = tensor.reshape(64 * 32, LANES)
    return pl.pallas_call(
        split_kernel,
        out_shape=jax.ShapeDtypeStruct((8, 64, 512), jnp.float32),
        compiler_params=pltpu.CompilerParams(vmem_limit_bytes=8 * 2**20),
    )(flat)


def dot_t(left, right):
    return lax.dot_general(left, right, (((1,), (1,)), ((), ())), preferred_element_type=jnp.float32)


def gram_kernel(f_ref, keep_ref, send_ref):
    full = f_ref[...]
    high = full.astype(jnp.bfloat16)
    low = (full - high.astype(jnp.float32)).astype(jnp.bfloat16)
    blocks = []
    for r in range(4):
        rows = slice(r * LANES, (r + 1) * LANES)
        n = (r + 1) * LANES
        part = dot_t(high[rows], high[:n]) + dot_t(high[rows], low[:n]) + dot_t(low[rows], high[:n])
        blocks += [part[:, c * LANES : (c + 1) * LANES] for c in range(r + 1)]
    core = lax.axis_index("core")
    for me in range(2):
        @pl.when(core == me)
        def _():
            for i, block in enumerate(blocks):
                ref = keep_ref if i // HALF == me else send_ref
                ref[i % HALF * LANES : (i % HALF + 1) * LANES, :] = block


def packed_gram(flat):
    half = jax.ShapeDtypeStruct((HALF * LANES, LANES), jnp.float32)
    return pl.pallas_call(
        gram_kernel, out_shape=(half, half), compiler_params=pltpu.CompilerParams(vmem_limit_bytes=12 * 2**20)
    )(flat)


def swap_cores(x):
    return lax.ppermute(x, "core", [(0, 1), (1, 0)])


def total_sum(keep, send):
    own = (keep + swap_cores(send)).reshape(32, 5, 4, LANES)
    own = lax.all_to_all(own, NEAR, 0, 0, tiled=True).sum(0)
    own = lax.all_to_all(jnp.broadcast_to(own, (8, 5, 4, LANES)), FAR, 0, 0, tiled=True).sum(0)
    own = lax.all_to_all(jnp.broadcast_to(own, (32, 5, 4, LANES)), NEAR, 0, 0, tiled=True)
    mine = own.reshape(HALF * LANES, LANES)
    return mine, swap_cores(mine)


def per_device(tensor, start_basis):
    regrouped = lax.all_to_all(split_columns(tensor), ("y", "core"), 0, 0, tiled=True)
    flat = regrouped.reshape(512, 512)
    factor, basis, core = chain(*total_sum(*packed_gram(flat)), start_basis, flat)
    return (factor, basis, core.reshape(128, 1, 512))


def solution(mesh):
    grid = Mesh(mesh.devices.reshape(4, 2, 8, 2, 4), ("y", "core", "z_high", "z_low", "x"))
    mode, col = ("y", "core"), ("z_high", "z_low", "x")
    in_specs = (P(mode, col, None), P())
    out_specs = (P(), P(), P(None, col, mode))
    return jax.shard_map(
        per_device, mesh=grid, in_specs=in_specs, out_specs=out_specs, check_vma=False
    )
```

```python
import functools

import jax
import jax.numpy as jnp
from jax import lax
from jax.experimental import pallas as pl
from jax.experimental.pallas import tpu as pltpu
from jax.sharding import Mesh, PartitionSpec as P

LANES = 128
BLOCKS = [(r, c) for r in range(4) for c in range(r + 1)]
HALF = len(BLOCKS) // 2
NEAR = ("y", "z_low", "x")
FAR = ("z_high",)
PER_F, PER_B = 2, 1
HIGHEST = lax.Precision.HIGHEST


def three(x):
    high = x.astype(jnp.bfloat16)
    rest = x - high.astype(jnp.float32)
    mid = rest.astype(jnp.bfloat16)
    low = (rest - mid.astype(jnp.float32)).astype(jnp.bfloat16)
    return high, mid, low


def left_of(h, m, l):
    return jnp.concatenate([h, h, m, h, l, m], 0)


def right_of(h, m, l):
    return jnp.concatenate([h, m, h, l, h, m], 0)


def parts(ref):
    return [ref[i * 32 : i * 32 + 32, :] for i in range(3)]


def dot_tn(left, right):
    return lax.dot_general(left, right, (((0,), (0,)), ((), ())), preferred_element_type=jnp.float32)


def lane(x, index):
    return jnp.take_along_axis(x, index, axis=1)


def row(x, k):
    return jnp.broadcast_to(x[k : k + 1, :], (8, LANES))


def eliminate(diag, groups, base, packed, result, per):
    diag, groups = list(diag), [list(g) for g in groups]
    zero = jnp.zeros((8, LANES), jnp.int32) + base
    for j0 in range(0, 4, per):
        inside = range(j0, j0 + per)
        cols = {}
        for c in range(8 * per):
            for i in range(j0 + c // 8, 4):
                cols[i, c] = lane(diag[i], zero + (8 * j0 + c))
        for j in inside:
            for v in range(len(groups[j])):
                packed[64 * j + 8 * v : 64 * j + 8 * v + 8, :] = groups[j][v]
            packed[64 * j + 32 : 64 * j + 40, :] = diag[j]
        rows = {c: packed[pl.ds(64 * (j0 + c // 8) + c % 8, 8, stride=8), :] for c in range(8 * per)}
        for c in range(8 * per):
            own = j0 + c // 8
            r = lax.rsqrt(row(cols[own, c], c % 8))
            low = {}
            for c2 in range(c + 1, 8 * per):
                low[c2] = row(cols[j0 + c2 // 8, c], c2 % 8) * r
            for i in range(own, 4):
                cols[i, c] = cols[i, c] * r
            rows[c] = rows[c] * r
            for c2 in range(c + 1, 8 * per):
                for i in range(j0 + c2 // 8, 4):
                    cols[i, c2] = cols[i, c2] - cols[i, c] * low[c2]
                rows[c2] = rows[c2] - rows[c] * low[c2]
            result[pl.ds(64 * own + c % 8, 8, stride=8), :] = rows[c]
            if j0 + per < 4:
                for v in [4, *range(len(groups[0]))]:
                    u = row(rows[c], v)
                    for i in range(j0 + per, 4):
                        if v == 4:
                            diag[i] = diag[i] - cols[i, c] * u
                        else:
                            groups[i][v] = groups[i][v] - cols[i, c] * u
            yield


def run(*steps):
    steps = list(steps)
    while steps:
        steps = [s for s in steps if next(s, True) is None]


def gathered(result, blocks):
    return jnp.concatenate([jnp.concatenate([result[64 * j + 8 * v : 64 * j + 8 * v + 8, :] for j in range(4)], 0) for v in blocks], 1)


def chain_kernel(
    mine_ref, other_ref, x_ref, f_ref, fac_out, basis_out, core_out,
    w, a_high, a_low, u, aug, ub, packed_f, result_f, packed_b, result_b, split_f, split_b, turned_f, turned_b,
    fac, basis, core, sems,
):
    core_index = lax.axis_index("core")
    for me in range(2):
        @pl.when(core_index == me)
        def _():
            for i, (r, c) in enumerate(BLOCKS):
                ref = mine_ref if i // HALF == me else other_ref
                block = ref[i % HALF * LANES : (i % HALF + 1) * LANES, :] * (1.0 / 262144)
                for x, (p, q) in [(block, (r, c))] + ([(block.T, (c, r))] if r != c else []):
                    rs, cs = slice(p * LANES, (p + 1) * LANES), slice(q * LANES, (q + 1) * LANES)
                    w[rs, cs] = x
                    a_high[rs, cs], a_low[rs, cs] = two(x)
    zero_all = [packed_f, packed_b, split_f, u]
    for ref in zero_all:
        ref[...] = jnp.zeros_like(ref)
    w[512:, :] = jnp.zeros((32, 512), jnp.float32)
    aug[LANES:, :] = jnp.zeros((32, 640), jnp.float32)
    ub[:, LANES:] = x_ref[...].T

    def near_update(target, start, across, rows, turned):
        lf = left_of(*three(across)).T
        turned[...] = lf
        offset = pl.multiple_of(lax.rem(start, LANES), 32)
        target[pl.ds(start, 32), :] -= jnp.dot(turned[pl.ds(offset, 32), :], rows, preferred_element_type=jnp.float32)

    def factor_step(s):
        start = pl.multiple_of(s * 32, 32)
        col = pl.multiple_of(s // 4 * LANES, LANES)
        diag = [w[pl.ds(start + 8 * i, 8), pl.ds(col, LANES)] for i in range(4)]
        groups = [[w[pl.ds(start + 8 * i, 8), v * LANES : (v + 1) * LANES] for v in range(1, 4)] for i in range(4)]
        before = parts(split_f)
        lf, rg = left_of(*before), right_of(*before)
        for r in range(4):
            w[r * LANES : (r + 1) * LANES, r * LANES :] -= dot_tn(lf[:, r * LANES : (r + 1) * LANES], rg[:, r * LANES :])
        yield from eliminate(diag, groups, lax.rem(s, 4) * 32, packed_f, result_f, PER_F)
        u[pl.ds(start, 32), LANES:] = gathered(result_f, range(3))
        u[pl.ds(start, 32), pl.ds(col, LANES)] = gathered(result_f, [4])
        now = three(u[pl.ds(start, 32), :])
        split_f[...] = jnp.concatenate(now, 0)
        nxt = pl.multiple_of(jnp.minimum((s + 1) // 4, 3) * LANES, LANES)
        near_update(w, pl.multiple_of(start + 32, 32), u[pl.ds(start, 32), pl.ds(nxt, LANES)], right_of(*now), turned_f)

    def basis_step(q):
        start = pl.multiple_of(q * 32, 32)
        groups = [[aug[pl.ds(start + 8 * i, 8), v * LANES : (v + 1) * LANES] for v in range(5)] for i in range(4)]
        before = parts(split_b)
        aug[:LANES, :] -= dot_tn(left_of(*before)[:, :LANES], right_of(*before))
        yield from eliminate([g[0] for g in groups], [g[1:] for g in groups], q * 32, packed_b, result_b, PER_B)
        rows = gathered(result_b, [4, 0, 1, 2, 3])
        ub[pl.ds(start, 32), :] = rows
        now = three(rows)
        split_b[...] = jnp.concatenate(now, 0)
        near_update(aug, pl.multiple_of(start + 32, 32), rows[:, :LANES], right_of(*now), turned_b)

    def finish(r):
        rows = slice(r * LANES, (r + 1) * LANES)
        for c in range(4):
            cols = slice(c * LANES, (c + 1) * LANES)
            if c > r:
                fac[rows, cols] = jnp.zeros((LANES, LANES), jnp.float32)
                continue
            block = u[cols, rows].T
            if c == r:
                lower = lax.broadcasted_iota(jnp.int32, (LANES, LANES), 0) >= lax.broadcasted_iota(jnp.int32, (LANES, LANES), 1)
                block = jnp.where(lower, block, 0.0)
            fac[rows, cols] = block
        copy = pltpu.make_async_copy(fac.at[rows], fac_out.at[rows], sems.at[r])
        copy.start()
        return copy

    def image_step():
        high, low = two(ub[:, LANES:])
        image = dot(high, a_high[...]) + dot(high, a_low[...]) + dot(low, a_high[...])
        split_b[...] = jnp.zeros_like(split_b)
        aug[:LANES, LANES:] = image
        aug[:LANES, :LANES] = lax.dot_general(image, image, (((1,), (1,)), ((), ())), precision=HIGHEST, preferred_element_type=jnp.float32)

    def power(t, carry):
        image_step()
        run(factor_step(5 * t))

        def both(q, c):
            run(factor_step(5 * t + 1 + q), basis_step(q))
            return c
        return lax.fori_loop(0, 4, both, carry)

    lax.fori_loop(0, 2, power, 0)
    basis_t = ub[:, LANES:]
    basis[...] = basis_t.T
    copies = [pltpu.make_async_copy(basis, basis_out, sems.at[4])]
    copies[-1].start()
    bh, bl = two(basis_t)
    fh, fl = two(f_ref[...])
    product = dot(bh, fh) + dot(bh, fl) + dot(bl, fh)
    for c in range(4):
        core[pl.ds(c, LANES, stride=4), :] = product[:, c * LANES : (c + 1) * LANES]
    copies.append(pltpu.make_async_copy(core, core_out, sems.at[5]))
    copies[-1].start()
    run(factor_step(10))
    copies += [finish(0), finish(1)]

    def rest(s, c):
        run(factor_step(s))
        return c
    lax.fori_loop(11, 16, rest, 0)
    copies += [finish(2), finish(3)]
    for copy in copies:
        copy.wait()


def two(x):
    high = x.astype(jnp.bfloat16)
    return high, (x - high.astype(jnp.float32)).astype(jnp.bfloat16)


def dot(left, right):
    return jnp.dot(left, right, preferred_element_type=jnp.float32)


def chain(mine, other, start_basis, flat):
    f32, b16 = jnp.float32, jnp.bfloat16
    return pl.pallas_call(
        chain_kernel,
        out_shape=(
            jax.ShapeDtypeStruct((512, 512), f32),
            jax.ShapeDtypeStruct((512, 128), f32),
            jax.ShapeDtypeStruct((512, 128), f32),
        ),
        out_specs=[pl.BlockSpec(memory_space=pl.ANY)] * 3,
        scratch_shapes=[
            pltpu.VMEM((544, 512), f32), pltpu.VMEM((512, 512), b16), pltpu.VMEM((512, 512), b16), pltpu.VMEM((512, 512), f32),
            pltpu.VMEM((160, 640), f32), pltpu.VMEM((128, 640), f32),
            *[pltpu.VMEM((256, LANES), f32)] * 4,
            pltpu.VMEM((96, 512), b16), pltpu.VMEM((96, 640), b16),
            pltpu.VMEM((128, 192), b16), pltpu.VMEM((128, 192), b16),
            pltpu.VMEM((512, 512), f32), pltpu.VMEM((512, 128), f32), pltpu.VMEM((512, 128), f32),
            pltpu.SemaphoreType.DMA((6,)),
        ],
        compiler_params=pltpu.CompilerParams(vmem_limit_bytes=24 * 2**20),
    )(mine, other, start_basis, flat)


def split_kernel(x_ref, o_ref):
    for d in range(8):
        for c in range(4):
            o_ref[d, :, c * LANES : (c + 1) * LANES] = x_ref[pl.ds(d * 4 + c, 64, stride=32), :]


def split_columns(tensor):
    flat = tensor.reshape(64 * 32, LANES)
    return pl.pallas_call(
        split_kernel,
        out_shape=jax.ShapeDtypeStruct((8, 64, 512), jnp.float32),
        compiler_params=pltpu.CompilerParams(vmem_limit_bytes=8 * 2**20),
    )(flat)


def dot_t(left, right):
    return lax.dot_general(left, right, (((1,), (1,)), ((), ())), preferred_element_type=jnp.float32)


def gram_kernel(f_ref, keep_ref, send_ref):
    full = f_ref[...]
    high = full.astype(jnp.bfloat16)
    low = (full - high.astype(jnp.float32)).astype(jnp.bfloat16)
    blocks = []
    for r in range(4):
        rows = slice(r * LANES, (r + 1) * LANES)
        n = (r + 1) * LANES
        part = dot_t(high[rows], high[:n]) + dot_t(high[rows], low[:n]) + dot_t(low[rows], high[:n])
        blocks += [part[:, c * LANES : (c + 1) * LANES] for c in range(r + 1)]
    core = lax.axis_index("core")
    for me in range(2):
        @pl.when(core == me)
        def _():
            for i, block in enumerate(blocks):
                ref = keep_ref if i // HALF == me else send_ref
                ref[i % HALF * LANES : (i % HALF + 1) * LANES, :] = block


def packed_gram(flat):
    half = jax.ShapeDtypeStruct((HALF * LANES, LANES), jnp.float32)
    return pl.pallas_call(
        gram_kernel, out_shape=(half, half), compiler_params=pltpu.CompilerParams(vmem_limit_bytes=12 * 2**20)
    )(flat)


def swap_cores(x):
    return lax.ppermute(x, "core", [(0, 1), (1, 0)])


def total_sum(keep, send):
    own = (keep + swap_cores(send)).reshape(32, 5, 4, LANES)
    own = lax.all_to_all(own, NEAR, 0, 0, tiled=True).sum(0)
    own = lax.all_to_all(jnp.broadcast_to(own, (8, 5, 4, LANES)), FAR, 0, 0, tiled=True).sum(0)
    own = lax.all_to_all(jnp.broadcast_to(own, (32, 5, 4, LANES)), NEAR, 0, 0, tiled=True)
    mine = own.reshape(HALF * LANES, LANES)
    return mine, swap_cores(mine)


def per_device(tensor, start_basis):
    regrouped = lax.all_to_all(split_columns(tensor), ("y", "core"), 0, 0, tiled=True)
    flat = regrouped.reshape(512, 512)
    factor, basis, core = chain(*total_sum(*packed_gram(flat)), start_basis, flat)
    return (factor, basis, core.reshape(128, 1, 512))


def solution(mesh):
    grid = Mesh(mesh.devices.reshape(4, 2, 8, 2, 4), ("y", "core", "z_high", "z_low", "x"))
    mode, col = ("y", "core"), ("z_high", "z_low", "x")
    in_specs = (P(mode, col, None), P())
    out_specs = (P(), P(), P(None, col, mode))
    return jax.shard_map(
        per_device, mesh=grid, in_specs=in_specs, out_specs=out_specs, check_vma=False
    )
```

```python
import functools

import jax
import jax.numpy as jnp
from jax import lax
from jax.experimental import pallas as pl
from jax.experimental.pallas import tpu as pltpu
from jax.sharding import Mesh, PartitionSpec as P

LANES = 128
BLOCKS = [(r, c) for r in range(4) for c in range(r + 1)]
HALF = len(BLOCKS) // 2
NEAR = ("y", "z_low", "x")
FAR = ("z_high",)
PER_F, PER_B = (2, 2, 2, 2), 1


def left_of(h, l):
    return jnp.concatenate([h, h, l], 0)


def right_of(h, l):
    return jnp.concatenate([h, l, h], 0)


def parts(ref):
    return [ref[i * 32 : i * 32 + 32, :] for i in range(2)]


def dot_tn(left, right):
    return lax.dot_general(left, right, (((0,), (0,)), ((), ())), preferred_element_type=jnp.float32)


def lane(x, index):
    return jnp.take_along_axis(x, index, axis=1)


def row(x, k):
    return jnp.broadcast_to(x[k : k + 1, :], (8, LANES))


def eliminate(diag, groups, base, packed, result, per):
    diag, groups = list(diag), [list(g) for g in groups]
    zero = jnp.zeros((8, LANES), jnp.int32) + base
    for j0 in range(0, 4, per):
        inside = range(j0, j0 + per)
        cols = {}
        for c in range(8 * per):
            for i in range(j0 + c // 8, 4):
                cols[i, c] = lane(diag[i], zero + (8 * j0 + c))
        for j in inside:
            for v in range(len(groups[j])):
                packed[64 * j + 8 * v : 64 * j + 8 * v + 8, :] = groups[j][v]
            packed[64 * j + 32 : 64 * j + 40, :] = diag[j]
        rows = {c: packed[pl.ds(64 * (j0 + c // 8) + c % 8, 8, stride=8), :] for c in range(8 * per)}
        for c in range(8 * per):
            own = j0 + c // 8
            r = lax.rsqrt(row(cols[own, c], c % 8))
            low = {}
            for c2 in range(c + 1, 8 * per):
                low[c2] = row(cols[j0 + c2 // 8, c], c2 % 8) * r
            for i in range(own, 4):
                cols[i, c] = cols[i, c] * r
            rows[c] = rows[c] * r
            for c2 in range(c + 1, 8 * per):
                for i in range(j0 + c2 // 8, 4):
                    cols[i, c2] = cols[i, c2] - cols[i, c] * low[c2]
                rows[c2] = rows[c2] - rows[c] * low[c2]
            result[pl.ds(64 * own + c % 8, 8, stride=8), :] = rows[c]
            if j0 + per < 4:
                for v in [4, *range(len(groups[0]))]:
                    u = row(rows[c], v)
                    for i in range(j0 + per, 4):
                        if v == 4:
                            diag[i] = diag[i] - cols[i, c] * u
                        else:
                            groups[i][v] = groups[i][v] - cols[i, c] * u
            yield


def run(*steps):
    steps = list(steps)
    while steps:
        steps = [s for s in steps if next(s, True) is None]


def gathered(result, blocks):
    return jnp.concatenate([jnp.concatenate([result[64 * j + 8 * v : 64 * j + 8 * v + 8, :] for j in range(4)], 0) for v in blocks], 1)


def chain_kernel(
    mine_ref, other_ref, x_ref, f_ref, fac_out, basis_out, core_out,
    w, a_high, a_low, u, aug, ub, packed_f, result_f, packed_b, result_b, split_f, split_b, turned_f, turned_b,
    fac, basis, core, sems,
):
    core_index = lax.axis_index("core")
    for me in range(2):
        @pl.when(core_index == me)
        def _():
            for i, (r, c) in enumerate(BLOCKS):
                ref = mine_ref if i // HALF == me else other_ref
                block = ref[i % HALF * LANES : (i % HALF + 1) * LANES, :] * (1.0 / 262144)
                for x, (p, q) in [(block, (r, c))] + ([(block.T, (c, r))] if r != c else []):
                    rs, cs = slice(p * LANES, (p + 1) * LANES), slice(q * LANES, (q + 1) * LANES)
                    w[rs, cs] = x
                    a_high[rs, cs], a_low[rs, cs] = two(x)
    zero_all = [packed_f, packed_b, split_f, u]
    for ref in zero_all:
        ref[...] = jnp.zeros_like(ref)
    w[512:, :] = jnp.zeros((32, 512), jnp.float32)
    aug[LANES:, :] = jnp.zeros((32, 640), jnp.float32)
    ub[:, LANES:] = x_ref[...].T

    def near_update(target, start, across, rows, turned, first):
        lf = left_of(*two(across)).T
        turned[...] = lf
        offset = pl.multiple_of(lax.rem(start, LANES), 32)
        target[pl.ds(start, 32), first * LANES :] -= jnp.dot(turned[pl.ds(offset, 32), :], rows, preferred_element_type=jnp.float32)

    def factor_step(s, first):
        start = pl.multiple_of(s * 32, 32)
        col = pl.multiple_of(s // 4 * LANES, LANES)
        diag = [w[pl.ds(start + 8 * i, 8), pl.ds(col, LANES)] for i in range(4)]
        groups = [[w[pl.ds(start + 8 * i, 8), v * LANES : (v + 1) * LANES] for v in range(first + 1, 4)] for i in range(4)]
        before = parts(split_f)
        lf, rg = left_of(*before), right_of(*before)
        for r in range(first, 4):
            w[r * LANES : (r + 1) * LANES, r * LANES :] -= dot_tn(lf[:, r * LANES : (r + 1) * LANES], rg[:, r * LANES :])
        yield from eliminate(diag, groups, lax.rem(s, 4) * 32, packed_f, result_f, PER_F[first])
        if first < 3:
            u[pl.ds(start, 32), (first + 1) * LANES :] = gathered(result_f, range(3 - first))
        u[pl.ds(start, 32), pl.ds(col, LANES)] = gathered(result_f, [4])
        now = two(u[pl.ds(start, 32), first * LANES :])
        split_f[:, first * LANES :] = jnp.concatenate(now, 0)
        nxt = pl.multiple_of(jnp.minimum((s + 1) // 4, 3) * LANES, LANES)
        near_update(w, pl.multiple_of(start + 32, 32), u[pl.ds(start, 32), pl.ds(nxt, LANES)], right_of(*now), turned_f, first)

    def basis_step(q):
        start = pl.multiple_of(q * 32, 32)
        groups = [[aug[pl.ds(start + 8 * i, 8), v * LANES : (v + 1) * LANES] for v in range(5)] for i in range(4)]
        before = parts(split_b)
        aug[:LANES, :] -= dot_tn(left_of(*before)[:, :LANES], right_of(*before))
        yield from eliminate([g[0] for g in groups], [g[1:] for g in groups], q * 32, packed_b, result_b, PER_B)
        rows = gathered(result_b, [4, 0, 1, 2, 3])
        ub[pl.ds(start, 32), :] = rows
        now = two(rows)
        split_b[...] = jnp.concatenate(now, 0)
        near_update(aug, pl.multiple_of(start + 32, 32), rows[:, :LANES], right_of(*now), turned_b, 0)

    def finish(r, first, last, sem):
        rows = slice(r * LANES, (r + 1) * LANES)
        for c in range(first, last):
            cols = slice(c * LANES, (c + 1) * LANES)
            if c > r:
                fac[rows, cols] = jnp.zeros((LANES, LANES), jnp.float32)
                continue
            block = u[cols, rows].T
            if c == r:
                lower = lax.broadcasted_iota(jnp.int32, (LANES, LANES), 0) >= lax.broadcasted_iota(jnp.int32, (LANES, LANES), 1)
                block = jnp.where(lower, block, 0.0)
            fac[rows, cols] = block
        cols = slice(first * LANES, last * LANES)
        copy = pltpu.make_async_copy(fac.at[rows, cols], fac_out.at[rows, cols], sems.at[sem])
        copy.start()
        return copy

    def image_step():
        high, low = two(ub[:, LANES:])
        image = dot(high, a_high[...]) + dot(high, a_low[...]) + dot(low, a_high[...])
        split_b[...] = jnp.zeros_like(split_b)
        aug[:LANES, LANES:] = image
        high, low = two(image)
        cross = dot_nt(high, low)
        aug[:LANES, :LANES] = dot_nt(high, high) + cross + cross.T

    for t in range(2):
        image_step()
        run(factor_step(5 * t, t))

        def both(q, c):
            run(basis_step(q), factor_step(5 * t + 1 + q, t))
            return c
        lax.fori_loop(0, 4, both, 0)

    basis_t = ub[:, LANES:]
    basis[...] = basis_t.T
    copies = [pltpu.make_async_copy(basis, basis_out, sems.at[4])]
    copies[-1].start()
    bh, bl = two(basis_t)
    fh, fl = two(f_ref[...])
    product = dot(bh, fh) + dot(bh, fl) + dot(bl, fh)
    for c in range(4):
        core[pl.ds(c, LANES, stride=4), :] = product[:, c * LANES : (c + 1) * LANES]
    copies.append(pltpu.make_async_copy(core, core_out, sems.at[5]))
    copies[-1].start()
    run(factor_step(10, 2))
    copies.append(finish(0, 0, 4, 0))
    run(factor_step(11, 2))
    copies.append(finish(1, 0, 4, 1))

    def rest(s, c):
        run(factor_step(s, 3))
        return c
    run(factor_step(12, 3))
    copies += [finish(2, 0, 4, 2), finish(3, 0, 3, 3)]
    lax.fori_loop(13, 16, rest, 0)
    copies.append(finish(3, 3, 4, 6))
    for copy in copies:
        copy.wait()


def two(x):
    high = x.astype(jnp.bfloat16)
    return high, (x - high.astype(jnp.float32)).astype(jnp.bfloat16)


def dot_nt(left, right):
    return lax.dot_general(left, right, (((1,), (1,)), ((), ())), preferred_element_type=jnp.float32)


def dot(left, right):
    return jnp.dot(left, right, preferred_element_type=jnp.float32)


def chain(mine, other, start_basis, flat):
    f32, b16 = jnp.float32, jnp.bfloat16
    return pl.pallas_call(
        chain_kernel,
        out_shape=(
            jax.ShapeDtypeStruct((512, 512), f32),
            jax.ShapeDtypeStruct((512, 128), f32),
            jax.ShapeDtypeStruct((512, 128), f32),
        ),
        out_specs=[pl.BlockSpec(memory_space=pl.ANY)] * 3,
        scratch_shapes=[
            pltpu.VMEM((544, 512), f32), pltpu.VMEM((512, 512), b16), pltpu.VMEM((512, 512), b16), pltpu.VMEM((512, 512), f32),
            pltpu.VMEM((160, 640), f32), pltpu.VMEM((128, 640), f32),
            *[pltpu.VMEM((256, LANES), f32)] * 4,
            pltpu.VMEM((64, 512), b16), pltpu.VMEM((64, 640), b16),
            pltpu.VMEM((128, 96), b16), pltpu.VMEM((128, 96), b16),
            pltpu.VMEM((512, 512), f32), pltpu.VMEM((512, 128), f32), pltpu.VMEM((512, 128), f32),
            pltpu.SemaphoreType.DMA((7,)),
        ],
        compiler_params=pltpu.CompilerParams(vmem_limit_bytes=24 * 2**20),
    )(mine, other, start_basis, flat)


def split_kernel(x_ref, o_ref):
    for d in range(8):
        for c in range(4):
            o_ref[d, :, c * LANES : (c + 1) * LANES] = x_ref[pl.ds(d * 4 + c, 64, stride=32), :]


def split_columns(tensor):
    flat = tensor.reshape(64 * 32, LANES)
    return pl.pallas_call(
        split_kernel,
        out_shape=jax.ShapeDtypeStruct((8, 64, 512), jnp.float32),
        compiler_params=pltpu.CompilerParams(vmem_limit_bytes=8 * 2**20),
    )(flat)


def dot_t(left, right):
    return lax.dot_general(left, right, (((1,), (1,)), ((), ())), preferred_element_type=jnp.float32)


def gram_kernel(f_ref, keep_ref, send_ref):
    full = f_ref[...]
    high = full.astype(jnp.bfloat16)
    low = (full - high.astype(jnp.float32)).astype(jnp.bfloat16)
    blocks = []
    for r in range(4):
        rows = slice(r * LANES, (r + 1) * LANES)
        n = (r + 1) * LANES
        part = dot_t(high[rows], high[:n]) + dot_t(high[rows], low[:n]) + dot_t(low[rows], high[:n])
        blocks += [part[:, c * LANES : (c + 1) * LANES] for c in range(r + 1)]
    core = lax.axis_index("core")
    for me in range(2):
        @pl.when(core == me)
        def _():
            for i, block in enumerate(blocks):
                ref = keep_ref if i // HALF == me else send_ref
                ref[i % HALF * LANES : (i % HALF + 1) * LANES, :] = block


def packed_gram(flat):
    half = jax.ShapeDtypeStruct((HALF * LANES, LANES), jnp.float32)
    return pl.pallas_call(
        gram_kernel, out_shape=(half, half), compiler_params=pltpu.CompilerParams(vmem_limit_bytes=12 * 2**20)
    )(flat)


def swap_cores(x):
    return lax.ppermute(x, "core", [(0, 1), (1, 0)])


def total_sum(keep, send):
    own = (keep + swap_cores(send)).reshape(32, 5, 4, LANES)
    own = lax.all_to_all(own, NEAR, 0, 0, tiled=True).sum(0)
    own = lax.all_to_all(jnp.broadcast_to(own, (8, 5, 4, LANES)), FAR, 0, 0, tiled=True).sum(0)
    own = lax.all_to_all(jnp.broadcast_to(own, (32, 5, 4, LANES)), NEAR, 0, 0, tiled=True)
    mine = own.reshape(HALF * LANES, LANES)
    return mine, swap_cores(mine)


def per_device(tensor, start_basis):
    regrouped = lax.all_to_all(split_columns(tensor), ("y", "core"), 0, 0, tiled=True)
    flat = regrouped.reshape(512, 512)
    factor, basis, core = chain(*total_sum(*packed_gram(flat)), start_basis, flat)
    return (factor, basis, core.reshape(128, 1, 512))


def solution(mesh):
    grid = Mesh(mesh.devices.reshape(4, 2, 8, 2, 4), ("y", "core", "z_high", "z_low", "x"))
    mode, col = ("y", "core"), ("z_high", "z_low", "x")
    in_specs = (P(mode, col, None), P())
    out_specs = (P(), P(), P(None, col, mode))
    return jax.shard_map(
        per_device, mesh=grid, in_specs=in_specs, out_specs=out_specs, check_vma=False
    )
```

```python
import functools

import jax
import jax.numpy as jnp
from jax import lax
from jax.experimental import pallas as pl
from jax.experimental.pallas import tpu as pltpu
from jax.sharding import Mesh, PartitionSpec as P

LANES = 128
BLOCKS = [(r, c) for r in range(4) for c in range(r + 1)]
HALF = len(BLOCKS) // 2
NEAR = ("y", "z_low", "x")
FAR = ("z_high",)
PER_F, PER_B = (2, 2, 2, 2), 1


def left_of(h, l):
    return jnp.concatenate([h, h, l], 0)


def right_of(h, l):
    return jnp.concatenate([h, l, h], 0)


def parts(ref):
    return [ref[i * 32 : i * 32 + 32, :] for i in range(2)]


def dot_tn(left, right):
    return lax.dot_general(left, right, (((0,), (0,)), ((), ())), preferred_element_type=jnp.float32)


def lane(x, index):
    return jnp.take_along_axis(x, index, axis=1)


def row(x, k):
    return jnp.broadcast_to(x[k : k + 1, :], (8, LANES))


def eliminate(diag, groups, base, packed, result, per):
    diag, groups = list(diag), [list(g) for g in groups]
    zero = jnp.zeros((8, LANES), jnp.int32) + base
    for j0 in range(0, 4, per):
        inside = range(j0, j0 + per)
        cols = {}
        for c in range(8 * per):
            for i in range(j0 + c // 8, 4):
                cols[i, c] = lane(diag[i], zero + (8 * j0 + c))
        for j in inside:
            for v in range(len(groups[j])):
                packed[64 * j + 8 * v : 64 * j + 8 * v + 8, :] = groups[j][v]
            packed[64 * j + 32 : 64 * j + 40, :] = diag[j]
        rows = {c: packed[pl.ds(64 * (j0 + c // 8) + c % 8, 8, stride=8), :] for c in range(8 * per)}
        for c in range(8 * per):
            own = j0 + c // 8
            r = lax.rsqrt(row(cols[own, c], c % 8))
            low = {}
            for c2 in range(c + 1, 8 * per):
                low[c2] = row(cols[j0 + c2 // 8, c], c2 % 8) * r
            for i in range(own, 4):
                cols[i, c] = cols[i, c] * r
            rows[c] = rows[c] * r
            for c2 in range(c + 1, 8 * per):
                for i in range(j0 + c2 // 8, 4):
                    cols[i, c2] = cols[i, c2] - cols[i, c] * low[c2]
                rows[c2] = rows[c2] - rows[c] * low[c2]
            result[pl.ds(64 * own + c % 8, 8, stride=8), :] = rows[c]
            if j0 + per < 4:
                for v in [4, *range(len(groups[0]))]:
                    u = row(rows[c], v)
                    for i in range(j0 + per, 4):
                        if v == 4:
                            diag[i] = diag[i] - cols[i, c] * u
                        else:
                            groups[i][v] = groups[i][v] - cols[i, c] * u
            yield


def run(*steps):
    steps = list(steps)
    while steps:
        steps = [s for s in steps if next(s, True) is None]


def gathered(result, blocks):
    return jnp.concatenate([jnp.concatenate([result[64 * j + 8 * v : 64 * j + 8 * v + 8, :] for j in range(4)], 0) for v in blocks], 1)


def chain_kernel(
    mine_ref, other_ref, x_ref, f_ref, fac_out, basis_out, core_out,
    w, a_high, a_low, u, aug, ub, packed_f, result_f, packed_b, result_b, split_f, split_b, turned_f, turned_b,
    fac, basis, core, sems,
):
    core_index = lax.axis_index("core")
    for me in range(2):
        @pl.when(core_index == me)
        def _():
            for i, (r, c) in enumerate(BLOCKS):
                ref = mine_ref if i // HALF == me else other_ref
                block = ref[i % HALF * LANES : (i % HALF + 1) * LANES, :] * (1.0 / 262144)
                for x, (p, q) in [(block, (r, c))] + ([(block.T, (c, r))] if r != c else []):
                    rs, cs = slice(p * LANES, (p + 1) * LANES), slice(q * LANES, (q + 1) * LANES)
                    w[rs, cs] = x
                    a_high[rs, cs], a_low[rs, cs] = two(x)
    zero_all = [packed_f, packed_b, split_f, u]
    for ref in zero_all:
        ref[...] = jnp.zeros_like(ref)
    w[512:, :] = jnp.zeros((32, 512), jnp.float32)
    aug[LANES:, :] = jnp.zeros((32, 640), jnp.float32)
    ub[:, LANES:] = x_ref[...].T

    def near_update(target, start, across, rows, turned, first):
        lf = left_of(*two(across)).T
        turned[...] = lf
        offset = pl.multiple_of(lax.rem(start, LANES), 32)
        target[pl.ds(start, 32), first * LANES :] -= jnp.dot(turned[pl.ds(offset, 32), :], rows, preferred_element_type=jnp.float32)

    def factor_step(s, first):
        start = pl.multiple_of(s * 32, 32)
        col = pl.multiple_of(s // 4 * LANES, LANES)
        diag = [w[pl.ds(start + 8 * i, 8), pl.ds(col, LANES)] for i in range(4)]
        groups = [[w[pl.ds(start + 8 * i, 8), v * LANES : (v + 1) * LANES] for v in range(first + 1, 4)] for i in range(4)]
        before = parts(split_f)
        lf, rg = left_of(*before), right_of(*before)
        for r in range(first, 4):
            w[r * LANES : (r + 1) * LANES, r * LANES :] -= dot_tn(lf[:, r * LANES : (r + 1) * LANES], rg[:, r * LANES :])
        yield from eliminate(diag, groups, lax.rem(s, 4) * 32, packed_f, result_f, PER_F[first])
        if first < 3:
            u[pl.ds(start, 32), (first + 1) * LANES :] = gathered(result_f, range(3 - first))
        u[pl.ds(start, 32), pl.ds(col, LANES)] = gathered(result_f, [4])
        now = two(u[pl.ds(start, 32), first * LANES :])
        split_f[:, first * LANES :] = jnp.concatenate(now, 0)
        nxt = pl.multiple_of(jnp.minimum((s + 1) // 4, 3) * LANES, LANES)
        near_update(w, pl.multiple_of(start + 32, 32), u[pl.ds(start, 32), pl.ds(nxt, LANES)], right_of(*now), turned_f, first)

    def basis_step(q):
        start = pl.multiple_of(q * 32, 32)
        groups = [[aug[pl.ds(start + 8 * i, 8), v * LANES : (v + 1) * LANES] for v in range(5)] for i in range(4)]
        before = parts(split_b)
        aug[:LANES, :] -= dot_tn(left_of(*before)[:, :LANES], right_of(*before))
        yield from eliminate([g[0] for g in groups], [g[1:] for g in groups], q * 32, packed_b, result_b, PER_B)
        rows = gathered(result_b, [4, 0, 1, 2, 3])
        ub[pl.ds(start, 32), :] = rows
        now = two(rows)
        split_b[...] = jnp.concatenate(now, 0)
        near_update(aug, pl.multiple_of(start + 32, 32), rows[:, :LANES], right_of(*now), turned_b, 0)

    def finish(r, first, last, sem):
        rows = slice(r * LANES, (r + 1) * LANES)
        for c in range(first, last):
            cols = slice(c * LANES, (c + 1) * LANES)
            if c > r:
                fac[rows, cols] = jnp.zeros((LANES, LANES), jnp.float32)
                continue
            block = u[cols, rows].T
            if c == r:
                lower = lax.broadcasted_iota(jnp.int32, (LANES, LANES), 0) >= lax.broadcasted_iota(jnp.int32, (LANES, LANES), 1)
                block = jnp.where(lower, block, 0.0)
            fac[rows, cols] = block
        cols = slice(first * LANES, last * LANES)
        copy = pltpu.make_async_copy(fac.at[rows, cols], fac_out.at[rows, cols], sems.at[sem])
        copy.start()
        return copy

    def image_step():
        high, low = two(ub[:, LANES:])
        image = dot(high, a_high[...]) + dot(high, a_low[...]) + dot(low, a_high[...])
        split_b[...] = jnp.zeros_like(split_b)
        aug[:LANES, LANES:] = image
        high, low = two(image)
        cross = dot_nt(high, low)
        aug[:LANES, :LANES] = dot_nt(high, high) + cross + cross.T

    for t in range(2):
        image_step()
        run(factor_step(5 * t, t))

        def both(q, c):
            run(basis_step(q), factor_step(5 * t + 1 + q, t))
            return c
        lax.fori_loop(0, 4, both, 0)

    basis_t = ub[:, LANES:]
    basis[...] = basis_t.T
    copies = [pltpu.make_async_copy(basis, basis_out, sems.at[4])]
    copies[-1].start()
    bh, bl = two(basis_t)
    fh, fl = two(f_ref[...])
    product = dot(bh, fh) + dot(bh, fl) + dot(bl, fh)
    for c in range(4):
        core[pl.ds(c, LANES, stride=4), :] = product[:, c * LANES : (c + 1) * LANES]
    copies.append(pltpu.make_async_copy(core, core_out, sems.at[5]))
    copies[-1].start()
    run(factor_step(10, 2))
    copies.append(finish(0, 0, 4, 0))
    run(factor_step(11, 2))
    copies.append(finish(1, 0, 4, 1))

    def rest(s, c):
        run(factor_step(s, 3))
        return c
    run(factor_step(12, 3))
    copies += [finish(2, 0, 4, 2), finish(3, 0, 3, 3)]
    lax.fori_loop(13, 16, rest, 0)
    copies.append(finish(3, 3, 4, 6))
    for copy in copies:
        copy.wait()


def two(x):
    high = x.astype(jnp.bfloat16)
    return high, (x - high.astype(jnp.float32)).astype(jnp.bfloat16)


def dot_nt(left, right):
    return lax.dot_general(left, right, (((1,), (1,)), ((), ())), preferred_element_type=jnp.float32)


def dot(left, right):
    return jnp.dot(left, right, preferred_element_type=jnp.float32)


def chain(mine, other, start_basis, flat):
    f32, b16 = jnp.float32, jnp.bfloat16
    return pl.pallas_call(
        chain_kernel,
        out_shape=(
            jax.ShapeDtypeStruct((512, 512), f32),
            jax.ShapeDtypeStruct((512, 128), f32),
            jax.ShapeDtypeStruct((512, 128), f32),
        ),
        out_specs=[pl.BlockSpec(memory_space=pl.ANY)] * 3,
        scratch_shapes=[
            pltpu.VMEM((544, 512), f32), pltpu.VMEM((512, 512), b16), pltpu.VMEM((512, 512), b16), pltpu.VMEM((512, 512), f32),
            pltpu.VMEM((160, 640), f32), pltpu.VMEM((128, 640), f32),
            *[pltpu.VMEM((256, LANES), f32)] * 4,
            pltpu.VMEM((64, 512), b16), pltpu.VMEM((64, 640), b16),
            pltpu.VMEM((128, 96), b16), pltpu.VMEM((128, 96), b16),
            pltpu.VMEM((512, 512), f32), pltpu.VMEM((512, 128), f32), pltpu.VMEM((512, 128), f32),
            pltpu.SemaphoreType.DMA((7,)),
        ],
        compiler_params=pltpu.CompilerParams(vmem_limit_bytes=24 * 2**20),
    )(mine, other, start_basis, flat)


def split_kernel(x_ref, o_ref):
    for d in range(8):
        for c in range(4):
            o_ref[d, :, c * LANES : (c + 1) * LANES] = x_ref[pl.ds(d * 4 + c, 64, stride=32), :]


def split_columns(tensor):
    flat = tensor.reshape(64 * 32, LANES)
    return pl.pallas_call(
        split_kernel,
        out_shape=jax.ShapeDtypeStruct((8, 64, 512), jnp.float32),
        compiler_params=pltpu.CompilerParams(vmem_limit_bytes=8 * 2**20),
    )(flat)


def dot_t(left, right):
    return lax.dot_general(left, right, (((1,), (1,)), ((), ())), preferred_element_type=jnp.float32)


def gram_kernel(f_ref, o_ref, *, kept):
    full = f_ref[...]
    high = full.astype(jnp.bfloat16)
    low = (full - high.astype(jnp.float32)).astype(jnp.bfloat16)
    core = lax.axis_index("core")
    for half in range(2):
        @pl.when((core == half) == kept)
        def _():
            blocks = BLOCKS[half * HALF : (half + 1) * HALF]
            at = 0
            for r in range(4):
                across = [c for row_block, c in blocks if row_block == r]
                if not across:
                    continue
                rows = slice(r * LANES, (r + 1) * LANES)
                cols = slice(across[0] * LANES, (across[-1] + 1) * LANES)
                part = dot_t(high[rows], high[cols]) + dot_t(high[rows], low[cols]) + dot_t(low[rows], high[cols])
                for i in range(len(across)):
                    o_ref[at : at + LANES, :] = part[:, i * LANES : (i + 1) * LANES]
                    at += LANES


def half_gram(flat, kept):
    return pl.pallas_call(
        functools.partial(gram_kernel, kept=kept),
        out_shape=jax.ShapeDtypeStruct((HALF * LANES, LANES), jnp.float32),
        compiler_params=pltpu.CompilerParams(vmem_limit_bytes=12 * 2**20),
        cost_estimate=pl.CostEstimate(flops=6 * 5 * 128 * 128 * 512, bytes_accessed=1400000, transcendentals=0),
    )(flat)


def swap_cores(x):
    return lax.ppermute(x, "core", [(0, 1), (1, 0)])


def total_sum(flat):
    came = swap_cores(half_gram(flat, False))
    own = (half_gram(flat, True) + came).reshape(32, 5, 4, LANES)
    own = lax.all_to_all(own, NEAR, 0, 0, tiled=True).sum(0)
    own = lax.all_to_all(jnp.broadcast_to(own, (8, 5, 4, LANES)), FAR, 0, 0, tiled=True).sum(0)
    own = lax.all_to_all(jnp.broadcast_to(own, (32, 5, 4, LANES)), NEAR, 0, 0, tiled=True)
    mine = own.reshape(HALF * LANES, LANES)
    return mine, swap_cores(mine)


def per_device(tensor, start_basis):
    regrouped = lax.all_to_all(split_columns(tensor), ("y", "core"), 0, 0, tiled=True)
    flat = regrouped.reshape(512, 512)
    factor, basis, core = chain(*total_sum(flat), start_basis, flat)
    return (factor, basis, core.reshape(128, 1, 512))


def solution(mesh):
    grid = Mesh(mesh.devices.reshape(4, 2, 8, 2, 4), ("y", "core", "z_high", "z_low", "x"))
    mode, col = ("y", "core"), ("z_high", "z_low", "x")
    in_specs = (P(mode, col, None), P())
    out_specs = (P(), P(), P(None, col, mode))
    return jax.shard_map(
        per_device, mesh=grid, in_specs=in_specs, out_specs=out_specs, check_vma=False
    )
```

```python
import functools

import jax
import jax.numpy as jnp
from jax import lax
from jax.experimental import pallas as pl
from jax.experimental.pallas import tpu as pltpu
from jax.sharding import Mesh, PartitionSpec as P

LANES = 128
BLOCKS = [(r, c) for r in range(4) for c in range(r + 1)]
HALF = len(BLOCKS) // 2
NEAR = ("x", "z_low", "y")
FAR = ("z_high",)
PER_F, PER_B = (2, 2, 2, 2), 1


def left_of(h, l):
    return jnp.concatenate([h, h, l], 0)


def right_of(h, l):
    return jnp.concatenate([h, l, h], 0)


def parts(ref):
    return [ref[i * 32 : i * 32 + 32, :] for i in range(2)]


def dot_tn(left, right):
    return lax.dot_general(left, right, (((0,), (0,)), ((), ())), preferred_element_type=jnp.float32)


def lane(x, index):
    return jnp.take_along_axis(x, index, axis=1)


def row(x, k):
    return jnp.broadcast_to(x[k : k + 1, :], (8, LANES))


def eliminate(diag, groups, base, packed, result, per):
    diag, groups = list(diag), [list(g) for g in groups]
    zero = jnp.zeros((8, LANES), jnp.int32) + base
    for j0 in range(0, 4, per):
        inside = range(j0, j0 + per)
        cols = {}
        for c in range(8 * per):
            for i in range(j0 + c // 8, 4):
                cols[i, c] = lane(diag[i], zero + (8 * j0 + c))
        for j in inside:
            for v in range(len(groups[j])):
                packed[64 * j + 8 * v : 64 * j + 8 * v + 8, :] = groups[j][v]
            packed[64 * j + 32 : 64 * j + 40, :] = diag[j]
        rows = {c: packed[pl.ds(64 * (j0 + c // 8) + c % 8, 8, stride=8), :] for c in range(8 * per)}
        for c in range(8 * per):
            own = j0 + c // 8
            r = lax.rsqrt(row(cols[own, c], c % 8))
            low = {}
            for c2 in range(c + 1, 8 * per):
                low[c2] = row(cols[j0 + c2 // 8, c], c2 % 8) * r
            for i in range(own, 4):
                cols[i, c] = cols[i, c] * r
            rows[c] = rows[c] * r
            for c2 in range(c + 1, 8 * per):
                for i in range(j0 + c2 // 8, 4):
                    cols[i, c2] = cols[i, c2] - cols[i, c] * low[c2]
                rows[c2] = rows[c2] - rows[c] * low[c2]
            result[pl.ds(64 * own + c % 8, 8, stride=8), :] = rows[c]
            if j0 + per < 4:
                for v in [4, *range(len(groups[0]))]:
                    u = row(rows[c], v)
                    for i in range(j0 + per, 4):
                        if v == 4:
                            diag[i] = diag[i] - cols[i, c] * u
                        else:
                            groups[i][v] = groups[i][v] - cols[i, c] * u
            yield


def run(*steps):
    steps = list(steps)
    while steps:
        steps = [s for s in steps if next(s, True) is None]


def gathered(result, blocks):
    return jnp.concatenate([jnp.concatenate([result[64 * j + 8 * v : 64 * j + 8 * v + 8, :] for j in range(4)], 0) for v in blocks], 1)


def chain_kernel(
    mine_ref, other_ref, x_ref, f_ref, fac_out, basis_out, core_out,
    w, a_high, a_low, u, aug, ub, packed_f, result_f, packed_b, result_b, split_f, split_b, turned_f, turned_b,
    fac, basis, core, sems,
):
    core_index = lax.axis_index("core")
    for me in range(2):
        @pl.when(core_index == me)
        def _():
            for i, (r, c) in enumerate(BLOCKS):
                ref = mine_ref if i // HALF == me else other_ref
                block = ref[i % HALF * LANES : (i % HALF + 1) * LANES, :] * (1.0 / 262144)
                for x, (p, q) in [(block, (r, c))] + ([(block.T, (c, r))] if r != c else []):
                    rs, cs = slice(p * LANES, (p + 1) * LANES), slice(q * LANES, (q + 1) * LANES)
                    w[rs, cs] = x
                    a_high[rs, cs], a_low[rs, cs] = two(x)
    zero_all = [packed_f, packed_b, split_f, u]
    for ref in zero_all:
        ref[...] = jnp.zeros_like(ref)
    w[512:, :] = jnp.zeros((32, 512), jnp.float32)
    aug[LANES:, :] = jnp.zeros((32, 640), jnp.float32)
    ub[:, LANES:] = x_ref[...].T

    def near_update(target, start, across, rows, turned, first):
        lf = left_of(*two(across)).T
        turned[...] = lf
        offset = pl.multiple_of(lax.rem(start, LANES), 32)
        target[pl.ds(start, 32), first * LANES :] -= jnp.dot(turned[pl.ds(offset, 32), :], rows, preferred_element_type=jnp.float32)

    def factor_step(s, first):
        start = pl.multiple_of(s * 32, 32)
        col = pl.multiple_of(s // 4 * LANES, LANES)
        diag = [w[pl.ds(start + 8 * i, 8), pl.ds(col, LANES)] for i in range(4)]
        groups = [[w[pl.ds(start + 8 * i, 8), v * LANES : (v + 1) * LANES] for v in range(first + 1, 4)] for i in range(4)]
        before = parts(split_f)
        lf, rg = left_of(*before), right_of(*before)
        for r in range(first, 4):
            w[r * LANES : (r + 1) * LANES, r * LANES :] -= dot_tn(lf[:, r * LANES : (r + 1) * LANES], rg[:, r * LANES :])
        yield from eliminate(diag, groups, lax.rem(s, 4) * 32, packed_f, result_f, PER_F[first])
        if first < 3:
            u[pl.ds(start, 32), (first + 1) * LANES :] = gathered(result_f, range(3 - first))
        u[pl.ds(start, 32), pl.ds(col, LANES)] = gathered(result_f, [4])
        now = two(u[pl.ds(start, 32), first * LANES :])
        split_f[:, first * LANES :] = jnp.concatenate(now, 0)
        nxt = pl.multiple_of(jnp.minimum((s + 1) // 4, 3) * LANES, LANES)
        near_update(w, pl.multiple_of(start + 32, 32), u[pl.ds(start, 32), pl.ds(nxt, LANES)], right_of(*now), turned_f, first)

    def basis_step(q):
        start = pl.multiple_of(q * 32, 32)
        groups = [[aug[pl.ds(start + 8 * i, 8), v * LANES : (v + 1) * LANES] for v in range(5)] for i in range(4)]
        before = parts(split_b)
        aug[:LANES, :] -= dot_tn(left_of(*before)[:, :LANES], right_of(*before))
        yield from eliminate([g[0] for g in groups], [g[1:] for g in groups], q * 32, packed_b, result_b, PER_B)
        rows = gathered(result_b, [4, 0, 1, 2, 3])
        ub[pl.ds(start, 32), :] = rows
        now = two(rows)
        split_b[...] = jnp.concatenate(now, 0)
        near_update(aug, pl.multiple_of(start + 32, 32), rows[:, :LANES], right_of(*now), turned_b, 0)

    def finish(r, first, last, sem):
        rows = slice(r * LANES, (r + 1) * LANES)
        for c in range(first, last):
            cols = slice(c * LANES, (c + 1) * LANES)
            if c > r:
                fac[rows, cols] = jnp.zeros((LANES, LANES), jnp.float32)
                continue
            block = u[cols, rows].T
            if c == r:
                lower = lax.broadcasted_iota(jnp.int32, (LANES, LANES), 0) >= lax.broadcasted_iota(jnp.int32, (LANES, LANES), 1)
                block = jnp.where(lower, block, 0.0)
            fac[rows, cols] = block
        cols = slice(first * LANES, last * LANES)
        copy = pltpu.make_async_copy(fac.at[rows, cols], fac_out.at[rows, cols], sems.at[sem])
        copy.start()
        return copy

    def image_step():
        high, low = two(ub[:, LANES:])
        image = dot(high, a_high[...]) + dot(high, a_low[...]) + dot(low, a_high[...])
        split_b[...] = jnp.zeros_like(split_b)
        aug[:LANES, LANES:] = image
        high, low = two(image)
        cross = dot_nt(high, low)
        aug[:LANES, :LANES] = dot_nt(high, high) + cross + cross.T

    for t in range(2):
        image_step()
        run(factor_step(5 * t, t))

        def both(q, c):
            run(basis_step(q), factor_step(5 * t + 1 + q, t))
            return c
        lax.fori_loop(0, 4, both, 0)

    basis_t = ub[:, LANES:]
    basis[...] = basis_t.T
    copies = [pltpu.make_async_copy(basis, basis_out, sems.at[4])]
    copies[-1].start()
    bh, bl = two(basis_t)
    fh, fl = two(f_ref[...])
    product = dot(bh, fh) + dot(bh, fl) + dot(bl, fh)
    for c in range(4):
        core[pl.ds(c, LANES, stride=4), :] = product[:, c * LANES : (c + 1) * LANES]
    copies.append(pltpu.make_async_copy(core, core_out, sems.at[5]))
    copies[-1].start()
    run(factor_step(10, 2))
    copies.append(finish(0, 0, 4, 0))
    run(factor_step(11, 2))
    copies.append(finish(1, 0, 4, 1))

    def rest(s, c):
        run(factor_step(s, 3))
        return c
    run(factor_step(12, 3))
    copies += [finish(2, 0, 4, 2), finish(3, 0, 3, 3)]
    lax.fori_loop(13, 16, rest, 0)
    copies.append(finish(3, 3, 4, 6))
    for copy in copies:
        copy.wait()


def two(x):
    high = x.astype(jnp.bfloat16)
    return high, (x - high.astype(jnp.float32)).astype(jnp.bfloat16)


def dot_nt(left, right):
    return lax.dot_general(left, right, (((1,), (1,)), ((), ())), preferred_element_type=jnp.float32)


def dot(left, right):
    return jnp.dot(left, right, preferred_element_type=jnp.float32)


def chain(mine, other, start_basis, flat):
    f32, b16 = jnp.float32, jnp.bfloat16
    return pl.pallas_call(
        chain_kernel,
        out_shape=(
            jax.ShapeDtypeStruct((512, 512), f32),
            jax.ShapeDtypeStruct((512, 128), f32),
            jax.ShapeDtypeStruct((512, 128), f32),
        ),
        out_specs=[pl.BlockSpec(memory_space=pl.ANY)] * 3,
        scratch_shapes=[
            pltpu.VMEM((544, 512), f32), pltpu.VMEM((512, 512), b16), pltpu.VMEM((512, 512), b16), pltpu.VMEM((512, 512), f32),
            pltpu.VMEM((160, 640), f32), pltpu.VMEM((128, 640), f32),
            *[pltpu.VMEM((256, LANES), f32)] * 4,
            pltpu.VMEM((64, 512), b16), pltpu.VMEM((64, 640), b16),
            pltpu.VMEM((128, 96), b16), pltpu.VMEM((128, 96), b16),
            pltpu.VMEM((512, 512), f32), pltpu.VMEM((512, 128), f32), pltpu.VMEM((512, 128), f32),
            pltpu.SemaphoreType.DMA((7,)),
        ],
        compiler_params=pltpu.CompilerParams(vmem_limit_bytes=24 * 2**20),
    )(mine, other, start_basis, flat)


def split_kernel(x_ref, o_ref):
    for d in range(8):
        for c in range(4):
            o_ref[d, :, c * LANES : (c + 1) * LANES] = x_ref[pl.ds(d * 4 + c, 64, stride=32), :]


def split_columns(tensor):
    flat = tensor.reshape(64 * 32, LANES)
    return pl.pallas_call(
        split_kernel,
        out_shape=jax.ShapeDtypeStruct((8, 64, 512), jnp.float32),
        compiler_params=pltpu.CompilerParams(vmem_limit_bytes=8 * 2**20),
    )(flat)


def dot_t(left, right):
    return lax.dot_general(left, right, (((1,), (1,)), ((), ())), preferred_element_type=jnp.float32)


def gram_kernel(f_ref, keep_ref, send_ref):
    full = f_ref[...]
    high = full.astype(jnp.bfloat16)
    low = (full - high.astype(jnp.float32)).astype(jnp.bfloat16)
    blocks = []
    for r in range(4):
        rows = slice(r * LANES, (r + 1) * LANES)
        n = (r + 1) * LANES
        part = dot_t(high[rows], high[:n]) + dot_t(high[rows], low[:n]) + dot_t(low[rows], high[:n])
        blocks += [part[:, c * LANES : (c + 1) * LANES] for c in range(r + 1)]
    core = lax.axis_index("core")
    for me in range(2):
        @pl.when(core == me)
        def _():
            for i, block in enumerate(blocks):
                ref = keep_ref if i // HALF == me else send_ref
                ref[i % HALF * LANES : (i % HALF + 1) * LANES, :] = block


def packed_gram(flat):
    half = jax.ShapeDtypeStruct((HALF * LANES, LANES), jnp.float32)
    return pl.pallas_call(
        gram_kernel, out_shape=(half, half), compiler_params=pltpu.CompilerParams(vmem_limit_bytes=12 * 2**20)
    )(flat)


def swap_cores(x):
    return lax.ppermute(x, "core", [(0, 1), (1, 0)])


def total_sum(keep, send):
    own = (keep + swap_cores(send)).reshape(32, 5, 4, LANES)
    own = lax.all_to_all(own, NEAR, 0, 0, tiled=True).sum(0)
    own = lax.all_to_all(jnp.broadcast_to(own, (8, 5, 4, LANES)), FAR, 0, 0, tiled=True).sum(0)
    own = lax.all_to_all(jnp.broadcast_to(own, (32, 5, 4, LANES)), NEAR, 0, 0, tiled=True)
    mine = own.reshape(HALF * LANES, LANES)
    return mine, swap_cores(mine)


def per_device(tensor, start_basis):
    regrouped = lax.all_to_all(split_columns(tensor), ("y", "core"), 0, 0, tiled=True)
    flat = regrouped.reshape(512, 512)
    factor, basis, core = chain(*total_sum(*packed_gram(flat)), start_basis, flat)
    return (factor, basis, core.reshape(128, 1, 512))


def solution(mesh):
    grid = Mesh(mesh.devices.reshape(4, 2, 8, 2, 4), ("y", "core", "z_high", "z_low", "x"))
    mode, col = ("y", "core"), ("z_high", "z_low", "x")
    in_specs = (P(mode, col, None), P())
    out_specs = (P(), P(), P(None, col, mode))
    return jax.shard_map(
        per_device, mesh=grid, in_specs=in_specs, out_specs=out_specs, check_vma=False
    )
```
